512 devices in a mesh: rows: 64 (over z, x, core), cols: 8 (over y).
Axes of the slice: x: 4, y: 8, z: 8, core: 2. Of those that a mesh axis runs over, the one named last changes fastest.
Arguments:
- cost: bfloat16 [28672, 28672], P('rows', 'cols'), may hold values from 0 to 1
- row_mass: float32 [28672], P('rows'), may hold values from 0.2 to 6
- col_mass: float32 [28672], P('cols'), may hold values from 0.2 to 6
- slab: bfloat16 [28672, 512], P('cols'), may hold values from -128 to 128
Outputs:
- aligned: bfloat16 [28672, 512], P('rows', 'cols')
The draws below stay inside these ranges and needn't reach their ends.
All inputs are finite; a program needn't handle non-finite values.
Results may differ from the reference program's by a relative error of at most 0.0058.
Values sent between devices are 32-bit elements; how exact they have to be, the bound alone decides.
A program may use at most 64 MiB of HBM per device.

```python
import math
import jax
import jax.numpy as jnp
from jax import lax

N1 = 28672
N2 = 28672
SLAB = 512
ITERS = 4


cluster_offset = 0.08


def cluster_labels(key):
    row_label = jax.random.uniform(jax.random.fold_in(key, 91), (N1,), jnp.float32)
    col_label = jax.random.uniform(jax.random.fold_in(key, 92), (N2,), jnp.float32)
    return (row_label, col_label)


def draw_cost(key, part):
    row_label, col_label = cluster_labels(key)
    key = jax.random.fold_in(key, 3)
    jitter = jax.random.uniform(key, (N1, N2), jnp.float32)
    crossing = jnp.abs(row_label[:, None] - col_label[None, :])
    return (cluster_offset * crossing + (1.0 - cluster_offset) * jitter).astype(jnp.bfloat16)


def draw_row_mass(key, part):
    row_label, col_label = cluster_labels(key)
    key = jax.random.fold_in(key, 4)
    uniform_draw = jax.random.uniform(key, (N1,), jnp.float32)
    base_mass = 0.2 * jnp.exp(math.log(15.0) * uniform_draw)
    return base_mass * (1.0 + row_label)


def draw_col_mass(key, part):
    row_label, col_label = cluster_labels(key)
    key = jax.random.fold_in(key, 5)
    uniform_draw = jax.random.uniform(key, (N2,), jnp.float32)
    base_mass = 0.2 * jnp.exp(math.log(15.0) * uniform_draw)
    return base_mass * (1.0 + (1.0 - col_label))


def raised(result, stream_key, source, target, parts, factor):
    owner, partner = [(jnp.arange(result.shape[position]) // (result.shape[position] // parts)).reshape([-1 if axis == position else 1 for axis in range(result.ndim)]) for position in (source, target)]
    chosen = jax.random.permutation(stream_key, parts)[partner]
    strong = (owner == chosen) | (owner == (partner + parts // 2) % parts)
    return jnp.where(strong, factor * result, result)


def block_scale(rng, shape, cuts, smallest, largest):
    level = 1.0
    for dim, blocks in cuts:
        draws = jax.random.uniform(jax.random.fold_in(jax.random.fold_in(rng, 6), dim), (blocks,), jnp.float32, smallest / len(cuts), largest / len(cuts))
        level = level * jnp.repeat(jnp.exp(draws), shape[dim] // blocks).reshape((-1,) + (1,) * (len(shape) - 1 - dim))
    return level


def heavy_noise(rng, extent, scale, most, pieces, heavy, held_as=jnp.bfloat16):
    drawn = scale * jax.random.normal(rng, extent, jnp.float32)
    if pieces:
        drawn = drawn * block_scale(rng, extent, pieces, -0.22, 0.18)
    return jnp.clip(raised(drawn, jax.random.fold_in(rng, 3), *heavy), -most, most).astype(held_as)


def setup_inputs(seed: int = 0) -> dict:
    seeds = jax.random.split(jax.random.key(seed), 5)
    return {
        "cost": draw_cost(jax.random.fold_in(seeds[4], 71), 0),
        "row_mass": draw_row_mass(jax.random.fold_in(seeds[4], 71), 0),
        "col_mass": draw_col_mass(jax.random.fold_in(seeds[4], 71), 0),
        "slab": heavy_noise(seeds[3], (N2, SLAB), 16.0, 128.0, ((0, 8),), (0, 1, 8, 2.0)),
    }


sharpness = 80.0


def kernel_of(tile_cost):
    rounded = jnp.exp(-sharpness * tile_cost.astype(jnp.float32)).astype(jnp.bfloat16)
    return lax.optimization_barrier(rounded)


def reference(cost, row_mass, col_mass, slab):
    height = 512 if N1 % 512 == 0 else N1
    block_count = N1 // height
    blocks = cost.reshape(block_count, height, N2)
    col_scale = jnp.ones((N2,), jnp.float32)
    row_scale = jnp.ones((N1,), jnp.float32)
    for repeat in range(ITERS):
        def row_block(tile_cost):
            return jnp.dot(kernel_of(tile_cost).astype(jnp.float32), col_scale, precision=lax.Precision.HIGHEST)

        row_sums = lax.map(row_block, blocks).reshape(N1)
        row_scale = row_mass / row_sums

        def accumulate(running, paired):
            tile_cost, tile_scale = paired
            added = jnp.dot(tile_scale, kernel_of(tile_cost).astype(jnp.float32), precision=lax.Precision.HIGHEST)
            return running + added, None

        col_sums, _ = lax.scan(accumulate, jnp.zeros((N2,), jnp.float32), (blocks, row_scale.reshape(block_count, height)))
        col_scale = col_mass / col_sums
    scaled = (col_scale[:, None] * slab.astype(jnp.float32)).astype(jnp.bfloat16)

    def slab_block(tile_cost):
        return jnp.dot(kernel_of(tile_cost), scaled, preferred_element_type=jnp.float32)

    product = lax.map(slab_block, blocks).reshape(N1, SLAB)
    return ((row_scale / row_mass)[:, None] * product).astype(jnp.bfloat16)
```

```python
import functools

import jax
import jax.numpy as jnp
from jax import lax
from jax.experimental import pallas as pl
from jax.experimental.pallas import tpu as pltpu
from jax.sharding import PartitionSpec as P

ITERS = 4
SHARPNESS = 80.0
MESH = pl.DeviceIdType.MESH
F32, BF16 = jnp.float32, jnp.bfloat16
NT = (((1,), (1,)), ((), ()))
TN = (((0,), (0,)), ((), ()))

ROWS, COLS, SLAB = 448, 3584, 512
NY = 8
OWN = SLAB // NY
CHUNKS = 2
CW = COLS // CHUNKS
TILES = CW // 128
TR = 16
LOADS = 7
LR = ROWS // LOADS
KC = 896
HALF = ROWS // 4
ORDER = (4, 3, 5, 2, 6, 1, 7)


def parent(s):
    return s + 1 if s < 0 else s - 1


def tree(h):
    left, right = (4, 3) if h == 0 else (3, 4)
    return [-s for s in range(left, 0, -1)] + list(range(right, 0, -1))


def split2(x):
    hi = x.astype(BF16).astype(F32)
    return hi, x - hi


def kernel(cost_ref, rm_ref, cm_ref, slab_ref, out_ref,
           k_ref, kr_ref, slab_v, acc_ref, t_ref, rbuf, racc, rb_ref, c2, left,
           ysrc, ydst, xsrc, xdst, zsrc, zdst,
           cost_sem, slab_sem, ysend, yrecv, xsend, xrecv, zsend, zrecv, fsend, frecv):
    r = lax.axis_index("rows")
    y = lax.axis_index("cols")
    lo = lax.rem(r, 8)

    def ypeer(d):
        return (r, lax.rem(y + d, 8))

    def xpeer(d):
        return (r - lo + lax.rem(lo + d, 8), y)

    def zpeer(d):
        return (lax.rem(r + 8 * d, 64), y)

    barrier = pltpu.get_barrier_semaphore()
    for peer in (ypeer, xpeer, zpeer):
        for d in ORDER:
            pl.semaphore_signal(barrier, inc=1, device_id=peer(d), device_id_type=MESH)

    def load(i):
        s = pl.ds(i * LR, LR)
        return pltpu.make_async_copy(cost_ref.at[s], k_ref.at[s], cost_sem.at[i])

    for i in range(LOADS):
        load(i).start()
    slab_copy = pltpu.make_async_copy(slab_ref, slab_v, slab_sem)
    slab_copy.start()

    left[...] = jnp.zeros_like(left)
    xsrc[...] = jnp.ones_like(xsrc)
    ysrc[...] = jnp.zeros_like(ysrc)

    for i in range(LOADS):
        load(i).wait()

        def exp_rows(j, carry, i=i):
            s = pl.ds(pl.multiple_of(i * LR + j * 32, 32), 32)
            k = jnp.exp(-SHARPNESS * k_ref[s, :].astype(F32)).astype(BF16)
            k_ref[s, :] = k
            k = k.astype(F32)
            total = k[:, 0:128]
            for q in range(1, COLS // 128):
                total = total + k[:, 128 * q:128 * (q + 1)]
            racc[s, :] = total
            return carry

        lax.fori_loop(0, LR // 32, exp_rows, 0)

    first = lax.dot_general(jnp.ones((8, 128), F32), racc[...], NT,
                            precision=lax.Precision.HIGHEST, preferred_element_type=F32)
    ysrc[0, :, 0:ROWS] = first[0:1]
    pl.semaphore_wait(barrier, 21)

    row8 = lax.broadcasted_iota(jnp.int32, (8, 1), 0)

    def two_rows(x):
        hi, rest = split2(x)
        return jnp.where(row8 == 0, hi, jnp.where(row8 == 1, rest, 0.0)).astype(BF16)

    def iteration(t, carry):
        for d in ORDER:
            pltpu.make_async_remote_copy(ysrc.at[t], ydst.at[t, d - 1], ysend.at[t], yrecv.at[t],
                                         device_id=ypeer(d), device_id_type=MESH).start()
        pltpu.make_async_copy(ydst.at[t], ydst.at[t], yrecv.at[t]).wait()
        sums = ysrc[t, :, 0:ROWS]
        for d in range(7):
            sums = sums + ydst[t, d, :, 0:ROWS]
        r2 = two_rows(rm_ref[...] / sums)

        for c in range(CHUNKS):
            part = jnp.dot(r2, k_ref[:, c * CW:(c + 1) * CW], preferred_element_type=F32)
            part = part[0:1] + part[1:2]
            for j in range(TILES):
                xsrc[t, c, j:j + 1, :] = part[:, 128 * j:128 * (j + 1)]
            for d in ORDER:
                pltpu.make_async_remote_copy(xsrc.at[t, c], xdst.at[t, c, d - 1], xsend.at[t], xrecv.at[t, c],
                                             device_id=xpeer(d), device_id_type=MESH).start()

        @pl.when(t == ITERS - 1)
        def _():
            r_over = two_rows(1.0 / sums)
            rb_ref[...] = lax.dot_general(r_over, jnp.ones((8, 128), BF16), TN, preferred_element_type=F32)

            def scale_rows(i, carry):
                s = pl.ds(pl.multiple_of(i * 32, 32), 32)
                rb = rb_ref[s, :]
                for q in range(COLS // 128):
                    kr_ref[s, 128 * q:128 * (q + 1)] = k_ref[s, 128 * q:128 * (q + 1)].astype(F32) * rb
                return carry

            lax.fori_loop(0, ROWS // 32, scale_rows, 0)

        for c in range(CHUNKS):
            pltpu.make_async_copy(xdst.at[t, c], xdst.at[t, c], xrecv.at[t, c]).wait()
            total = xsrc[t, c]
            for d in range(7):
                total = total + xdst[t, c, d]
            zsrc[t, c] = total
            for d in ORDER:
                pltpu.make_async_remote_copy(zsrc.at[t, c], zdst.at[t, c, d - 1], zsend.at[t], zrecv.at[t, c],
                                             device_id=zpeer(d), device_id_type=MESH).start()
        for c in range(CHUNKS):
            pltpu.make_async_copy(zdst.at[t, c], zdst.at[t, c], zrecv.at[t, c]).wait()
            total = zsrc[t, c]
            for d in range(7):
                total = total + zdst[t, c, d]
            scale = cm_ref[c] / total
            hi, rest = split2(scale)
            c2[0] = hi
            c2[1] = rest
            for j in range(TILES):
                lanes = pl.ds(c * CW + 128 * j, 128)
                left[0:1, lanes] = c2[0, j:j + 1, :]
                left[1:2, lanes] = c2[1, j:j + 1, :]

        @pl.when(t < ITERS - 1)
        def _():
            sums = jnp.zeros((8, ROWS), F32)
            for c in range(CHUNKS):
                s = slice(c * CW, (c + 1) * CW)
                sums = sums + lax.dot_general(left[:, s].astype(BF16), k_ref[:, s], NT, preferred_element_type=F32)
            ysrc[t + 1, :, 0:ROWS] = sums[0:1] + sums[1:2]

        return carry

    lax.fori_loop(0, ITERS, iteration, 0)

    slab_copy.wait()
    acc_ref[...] = jnp.zeros_like(acc_ref)

    def product(i, carry):
        s = pl.ds(pl.multiple_of(i * KC, KC), KC)
        scale = left[0:1, s] + left[1:2, s]
        plan = (kr_ref[:, s] * scale).astype(BF16)
        acc_ref[...] += jnp.dot(plan, slab_v[s, :], preferred_element_type=F32)
        return carry

    lax.fori_loop(0, COLS // KC, product, 0)

    def pack(i, carry):
        rows = pl.ds(pl.multiple_of(i * 32, 32), 32)
        below = pl.ds(pl.multiple_of(i * 32 + ROWS // 2, 32), 32)
        for p in range(NY // 2):
            lanes = slice(128 * p, 128 * (p + 1))
            top, bottom = acc_ref[rows, lanes], acc_ref[below, lanes]
            t_ref[2 * p, rows, :] = jnp.concatenate([top[:, :OWN], bottom[:, :OWN]], axis=1)
            t_ref[2 * p + 1, rows, :] = jnp.concatenate([top[:, OWN:], bottom[:, OWN:]], axis=1)
        return carry

    lax.fori_loop(0, ROWS // 64, pack, 0)

    nodes = [(h, s) for m in (4, 3, 2, 1) for h in (0, 1) for s in tree(h) if abs(s) == m]

    def slot(h, s):
        return tree(h).index(s)

    def hop(h, s):
        rows = pl.ds(h * HALF, HALF)
        dest = lax.rem(y - s + 8, 8)
        return pltpu.make_async_remote_copy(
            t_ref.at[dest, rows], rbuf.at[h, slot(h, s)], fsend.at[h, slot(h, s)], frecv.at[h, slot(h, s)],
            device_id=ypeer((parent(s) - s) % 8), device_id_type=MESH)

    def arrived(h, s):
        pltpu.make_async_copy(rbuf.at[h, slot(h, s)], rbuf.at[h, slot(h, s)], frecv.at[h, slot(h, s)]).wait()

    for h, s in nodes:
        rows = slice(h * HALF, (h + 1) * HALF)
        dest = lax.rem(y - s + 8, 8)
        for child in tree(h):
            if parent(child) == s:
                arrived(h, child)
                t_ref[dest, rows, :] = t_ref[dest, rows, :] + rbuf[h, slot(h, child)]
        hop(h, s).start()
    for h in (0, 1):
        rows = slice(h * HALF, (h + 1) * HALF)
        total = t_ref[y, rows, :]
        for child in tree(h):
            if parent(child) == 0:
                arrived(h, child)
                total = total + rbuf[h, slot(h, child)]
        total = total.astype(BF16)
        out_ref[h * HALF:(h + 1) * HALF, :] = total[:, :OWN]
        out_ref[ROWS // 2 + h * HALF:ROWS // 2 + (h + 1) * HALF, :] = total[:, OWN:]

    for t in range(ITERS):
        pltpu.make_async_copy(ydst.at[t], ydst.at[t], ysend.at[t]).wait()
        pltpu.make_async_copy(xdst.at[t], xdst.at[t], xsend.at[t]).wait()
        pltpu.make_async_copy(zdst.at[t], zdst.at[t], zsend.at[t]).wait()
    for h, s in nodes:
        hop(h, s).wait_send()


def on_device(cost, row_mass, col_mass, slab):
    masses = col_mass.reshape(CHUNKS, TILES, 128)
    masses = jnp.pad(masses, ((0, 0), (0, TR - TILES), (0, 0)), constant_values=1.0)
    vmem = pl.BlockSpec(memory_space=pltpu.VMEM)
    hbm = pl.BlockSpec(memory_space=pl.ANY)
    dma = pltpu.SemaphoreType.DMA
    return pl.pallas_call(
        kernel,
        out_shape=jax.ShapeDtypeStruct((ROWS, OWN), BF16),
        in_specs=[hbm, vmem, vmem, hbm],
        out_specs=vmem,
        scratch_shapes=[
            pltpu.VMEM((ROWS, COLS), BF16),
            pltpu.VMEM((ROWS, COLS), F32),
            pltpu.VMEM((COLS, SLAB), BF16),
            pltpu.VMEM((ROWS, SLAB), F32),
            pltpu.VMEM((NY, ROWS // 2, 128), F32),
            pltpu.VMEM((2, 7, HALF, 128), F32),
            pltpu.VMEM((ROWS, 128), F32),
            pltpu.VMEM((ROWS, 128), F32),
            pltpu.VMEM((2, TR, 128), F32),
            pltpu.VMEM((8, COLS), F32),
            pltpu.VMEM((ITERS, 1, 512), F32),
            pltpu.VMEM((ITERS, 7, 1, 512), F32),
            pltpu.VMEM((ITERS, CHUNKS, TR, 128), F32),
            pltpu.VMEM((ITERS, CHUNKS, 7, TR, 128), F32),
            pltpu.VMEM((ITERS, CHUNKS, TR, 128), F32),
            pltpu.VMEM((ITERS, CHUNKS, 7, TR, 128), F32),
            dma((LOADS,)), dma,
            dma((ITERS,)), dma((ITERS,)),
            dma((ITERS,)), dma((ITERS, CHUNKS)),
            dma((ITERS,)), dma((ITERS, CHUNKS)),
            dma((2, 7)), dma((2, 7)),
        ],
        compiler_params=pltpu.CompilerParams(
            collective_id=0, has_side_effects=True, vmem_limit_bytes=48 * 2**20),
    )(cost, row_mass.reshape(1, ROWS), masses, slab)


def solution(mesh):
    return jax.shard_map(
        on_device,
        mesh=mesh,
        in_specs=(P("rows", "cols"), P("rows"), P("cols"), P("cols", None)),
        out_specs=P("rows", "cols"),
        check_vma=False,
    )
```

```python
import functools

import jax
import jax.numpy as jnp
from jax import lax
from jax.experimental import pallas as pl
from jax.experimental.pallas import tpu as pltpu
from jax.sharding import PartitionSpec as P

ITERS = 4
SHARPNESS = 80.0
MESH = pl.DeviceIdType.MESH
F32, BF16 = jnp.float32, jnp.bfloat16
NT = (((1,), (1,)), ((), ()))
TN = (((0,), (0,)), ((), ()))

ROWS, COLS, SLAB = 448, 3584, 512
NY = 8
OWN = SLAB // NY
CW = COLS // 2
TILES = CW // 128
TR = 16
LOADS = 7
LR = ROWS // LOADS
KC = 896
PR = ROWS // 8
ORDER = (4, 3, 5, 2, 6, 1, 7)
GROUP = tuple((other, dx, dz) for other in (0, 1) for dx, dz in
              ((2, 1), (2, 0), (1, 1), (3, 1), (1, 0), (3, 0), (0, 1), (0, 0)) if (other, dx, dz) != (0, 0, 0))


def parent(s):
    if abs(s) == 4:
        return s // 2
    return s + 1 if s < 0 else s - 1


def tree(p):
    left, right = (4, 3) if p % 2 == 0 else (3, 4)
    return [-s for s in range(left, 0, -1)] + list(range(right, 0, -1))


def split2(x):
    hi = x.astype(BF16).astype(F32)
    return hi, x - hi


def kernel(cost_ref, rm_hbm, cm_hbm, slab_ref, out_ref,
           k_ref, kr_ref, slab_v, acc_ref, t_ref, rbuf, racc, rb_ref, c2, left, rm_ref, cm_row, cm_ref,
           ysrc, ydst, xsrc, xdst, zsrc, zdst,
           cost_sem, slab_sem, mass_sem, ysend, yrecv, xsend, xrecv, zsend, zrecv, fsend, frecv):
    r = lax.axis_index("rows")
    y = lax.axis_index("cols")
    z = r // 8
    x = lax.rem(r, 8) // 2
    core = lax.rem(r, 2)
    odd = lax.rem(z, 2)
    sign = 2 * odd - 1

    def ypeer(d):
        return (r, lax.rem(y + d, 8))

    def place(to_z, to_x, to_core):
        return (to_z * 8 + to_x * 2 + to_core, y)

    def gpeer(other, dx, dz):
        to_core = core + other * (1 - 2 * core)
        return place(z - dz * sign, lax.rem(x + dx, 4), to_core)

    def zpeer(other, k):
        to_core = core + other * (1 - 2 * core)
        return place(lax.rem(z + k * sign + 8, 8), x, to_core)

    barrier = pltpu.get_barrier_semaphore()

    def greet(peer):
        pl.semaphore_signal(barrier, inc=1, device_id=peer, device_id_type=MESH)

    for d in ORDER:
        greet(ypeer(d))
    for other, dx, dz in GROUP:
        greet(gpeer(other, dx, dz))
    for k in (1, 2, 3, -2):
        for other in (0, 1):
            greet(zpeer(other, k))

    def load(i):
        s = pl.ds(i * LR, LR)
        return pltpu.make_async_copy(cost_ref.at[s], k_ref.at[s], cost_sem.at[i])

    for i in range(LOADS):
        load(i).start()
    rm_copy = pltpu.make_async_copy(rm_hbm, rm_ref, mass_sem.at[0])
    cm_copy = pltpu.make_async_copy(cm_hbm, cm_row, mass_sem.at[1])
    slab_copy = pltpu.make_async_copy(slab_ref, slab_v, slab_sem)
    rm_copy.start()
    cm_copy.start()
    slab_copy.start()

    left[...] = jnp.zeros_like(left)
    xsrc[...] = jnp.ones_like(xsrc)
    ysrc[...] = jnp.zeros_like(ysrc)
    cm_ref[...] = jnp.ones_like(cm_ref)

    for i in range(LOADS):
        load(i).wait()

        def exp_rows(j, carry, i=i):
            s = pl.ds(pl.multiple_of(i * LR + j * 32, 32), 32)
            k = jnp.exp(-SHARPNESS * k_ref[s, :].astype(F32)).astype(BF16)
            k_ref[s, :] = k
            k = k.astype(F32)
            total = k[:, 0:128]
            for q in range(1, COLS // 128):
                total = total + k[:, 128 * q:128 * (q + 1)]
            racc[s, :] = total
            return carry

        lax.fori_loop(0, LR // 32, exp_rows, 0)

    first = lax.dot_general(jnp.ones((8, 128), F32), racc[...], NT,
                            precision=lax.Precision.HIGHEST, preferred_element_type=F32)
    ysrc[0, :, 0:ROWS] = first[0:1]
    pl.semaphore_wait(barrier, 7 + len(GROUP) + 8)
    rm_copy.wait()
    cm_copy.wait()

    row8 = lax.broadcasted_iota(jnp.int32, (8, 1), 0)

    def two_rows(v):
        hi, rest = split2(v)
        return jnp.where(row8 == 0, hi, jnp.where(row8 == 1, rest, 0.0)).astype(BF16)

    def iteration(t, carry):
        for d in ORDER:
            pltpu.make_async_remote_copy(ysrc.at[t], ydst.at[t, d - 1], ysend.at[t], yrecv.at[t],
                                         device_id=ypeer(d), device_id_type=MESH).start()

        @pl.when(t == 0)
        def _():
            for h in range(2):
                for j in range(TILES):
                    cm_ref[h, j:j + 1, :] = cm_row[pl.ds(h * CW + 128 * j, 128)].reshape(1, 128)

        pltpu.make_async_copy(ydst.at[t], ydst.at[t], yrecv.at[t]).wait()
        sums = ysrc[t, :, 0:ROWS]
        for d in range(7):
            sums = sums + ydst[t, d, :, 0:ROWS]
        r2 = two_rows(rm_ref[...] / sums)

        for other in (1, 0):
            h = core + other * (1 - 2 * core)
            part = jnp.dot(r2, k_ref[:, pl.ds(pl.multiple_of(h * CW, CW), CW)], preferred_element_type=F32)
            part = part[0:1] + part[1:2]
            for j in range(TILES):
                xsrc[t, other, j:j + 1, :] = part[:, 128 * j:128 * (j + 1)]
            for to, dx, dz in GROUP:
                if to == other:
                    pltpu.make_async_remote_copy(
                        xsrc.at[t, other], xdst.at[t, GROUP.index((to, dx, dz))], xsend.at[t], xrecv.at[t],
                        device_id=gpeer(to, dx, dz), device_id_type=MESH).start()

        @pl.when(t == ITERS - 1)
        def _():
            r_over = two_rows(1.0 / sums)
            rb_ref[...] = lax.dot_general(r_over, jnp.ones((8, 128), BF16), TN, preferred_element_type=F32)

            def scale_rows(i, carry):
                s = pl.ds(pl.multiple_of(i * 32, 32), 32)
                rb = rb_ref[s, :]
                for q in range(COLS // 128):
                    kr_ref[s, 128 * q:128 * (q + 1)] = k_ref[s, 128 * q:128 * (q + 1)].astype(F32) * rb
                return carry

            lax.fori_loop(0, ROWS // 32, scale_rows, 0)

        pltpu.make_async_copy(xdst.at[t], xdst.at[t], xrecv.at[t]).wait()
        total = xsrc[t, 0]
        for i in range(len(GROUP)):
            total = total + xdst[t, i]
        zsrc[t] = total
        for k, other in ((3, 1), (3, 0), (2, 1), (2, 0), (1, 1), (1, 0), (0, 1)):
            pltpu.make_async_remote_copy(zsrc.at[t], zdst.at[t, other, k], zsend.at[t], zrecv.at[t, other],
                                         device_id=zpeer(other, k), device_id_type=MESH).start()
        sums = jnp.zeros((8, ROWS), F32)
        for other in (0, 1):
            h = core + other * (1 - 2 * core)
            here = zdst.at[t, other, pl.ds(1 - other, 3 + other)]
            pltpu.make_async_copy(here, here, zrecv.at[t, other]).wait()
            total = zdst[t, other, 0] if other else zsrc[t]
            for k in (1, 2, 3):
                total = total + zdst[t, other, k]
            hi, rest = split2(cm_ref[h] / total)
            c2[0] = hi
            c2[1] = rest
            for j in range(TILES):
                lanes = pl.ds(pl.multiple_of(h * CW + 128 * j, 128), 128)
                left[0:1, lanes] = c2[0, j:j + 1, :]
                left[1:2, lanes] = c2[1, j:j + 1, :]
            lanes = pl.ds(pl.multiple_of(h * CW, CW), CW)
            part = lax.dot_general(left[:, lanes].astype(BF16), k_ref[:, lanes], NT, preferred_element_type=F32)
            if other == 0:
                sums = part
            else:
                sums = sums + part

        @pl.when(t < ITERS - 1)
        def _():
            ysrc[t + 1, :, 0:ROWS] = sums[0:1] + sums[1:2]

        return carry

    lax.fori_loop(0, ITERS, iteration, 0)

    def hop(p, s):
        i = tree(p).index(s)
        dest = lax.rem(y - s + 8, 8)
        return pltpu.make_async_remote_copy(
            t_ref.at[dest, pl.ds(p * PR, PR)], rbuf.at[p, i], fsend.at[p, i], frecv.at[p, i],
            device_id=ypeer((parent(s) - s) % 8), device_id_type=MESH)

    def add_arrived(p, s, total):
        for child in tree(p):
            if parent(child) == s:
                i = tree(p).index(child)
                pltpu.make_async_copy(rbuf.at[p, i], rbuf.at[p, i], frecv.at[p, i]).wait()
                total = total + rbuf[p, i]
        return total

    slab_copy.wait()
    for h in (0, 1):
        top = h * ROWS // 2

        def product(i, carry, top=top):
            s = pl.ds(pl.multiple_of(i * KC, KC), KC)
            scale = left[0:1, s] + left[1:2, s]
            plan = (kr_ref[top:top + ROWS // 2, s] * scale).astype(BF16)
            part = jnp.dot(plan, slab_v[s, :], preferred_element_type=F32)

            @pl.when(i == 0)
            def _():
                acc_ref[...] = part

            @pl.when(i > 0)
            def _():
                acc_ref[...] += part

            return carry

        lax.fori_loop(0, COLS // KC, product, 0)

        def pack(i, carry, h=h):
            rows = pl.ds(pl.multiple_of(i * 16, 16), 16)
            below = pl.ds(pl.multiple_of(i * 16 + ROWS // 4, 16), 16)
            to = pl.ds(pl.multiple_of(h * (ROWS // 4) + i * 16, 16), 16)
            for p in range(NY // 2):
                lanes = slice(128 * p, 128 * (p + 1))
                upper, lower = acc_ref[rows, lanes], acc_ref[below, lanes]
                t_ref[2 * p, to, :] = jnp.concatenate([upper[:, :OWN], lower[:, :OWN]], axis=1)
                t_ref[2 * p + 1, to, :] = jnp.concatenate([upper[:, OWN:], lower[:, OWN:]], axis=1)
            return carry

        lax.fori_loop(0, ROWS // 64, pack, 0)
        for m in (4, 3):
            for p in (2 * h, 2 * h + 1):
                for s in (-m, m):
                    if s in tree(p):
                        hop(p, s).start()

    for m in (2, 1):
        for p in range(4):
            for s in (-m, m):
                rows = slice(p * PR, (p + 1) * PR)
                dest = lax.rem(y - s + 8, 8)
                t_ref[dest, rows, :] = add_arrived(p, s, t_ref[dest, rows, :])
                hop(p, s).start()
    for p in range(4):
        total = add_arrived(p, 0, t_ref[y, p * PR:(p + 1) * PR, :]).astype(BF16)
        top = (p // 2) * (ROWS // 2) + (p % 2) * PR
        out_ref[top:top + PR, :] = total[:, :OWN]
        out_ref[top + ROWS // 4:top + ROWS // 4 + PR, :] = total[:, OWN:]

    for t in range(ITERS):
        pltpu.make_async_copy(ydst.at[t], ydst.at[t], ysend.at[t]).wait()
        pltpu.make_async_copy(xdst.at[t], xdst.at[t], xsend.at[t]).wait()
        sent = zdst.at[t, 0, pl.ds(1, 3)]
        pltpu.make_async_copy(sent, sent, zsend.at[t]).wait()
        pltpu.make_async_copy(zdst.at[t, 1], zdst.at[t, 1], zsend.at[t]).wait()
    for p in range(4):
        for s in tree(p):
            hop(p, s).wait_send()


def on_device(cost, row_mass, col_mass, slab):
    hbm = pl.BlockSpec(memory_space=pltpu.HBM)
    dma = pltpu.SemaphoreType.DMA
    return pl.pallas_call(
        kernel,
        out_shape=jax.ShapeDtypeStruct((ROWS, OWN), BF16),
        in_specs=[hbm, hbm, hbm, hbm],
        out_specs=pl.BlockSpec(memory_space=pltpu.VMEM),
        scratch_shapes=[
            pltpu.VMEM((ROWS, COLS), BF16),
            pltpu.VMEM((ROWS, COLS), F32),
            pltpu.VMEM((COLS, SLAB), BF16),
            pltpu.VMEM((ROWS // 2, SLAB), F32),
            pltpu.VMEM((NY, ROWS // 2, 128), F32),
            pltpu.VMEM((4, 7, PR, 128), F32),
            pltpu.VMEM((ROWS, 128), F32),
            pltpu.VMEM((ROWS, 128), F32),
            pltpu.VMEM((2, TR, 128), F32),
            pltpu.VMEM((8, COLS), F32),
            pltpu.VMEM((1, ROWS), F32),
            pltpu.VMEM((COLS,), F32),
            pltpu.VMEM((2, TR, 128), F32),
            pltpu.VMEM((ITERS, 1, 512), F32),
            pltpu.VMEM((ITERS, 7, 1, 512), F32),
            pltpu.VMEM((ITERS, 2, TR, 128), F32),
            pltpu.VMEM((ITERS, len(GROUP), TR, 128), F32),
            pltpu.VMEM((ITERS, TR, 128), F32),
            pltpu.VMEM((ITERS, 2, 4, TR, 128), F32),
            dma((LOADS,)), dma, dma((2,)),
            dma((ITERS,)), dma((ITERS,)),
            dma((ITERS,)), dma((ITERS,)),
            dma((ITERS,)), dma((ITERS, 2)),
            dma((4, 7)), dma((4, 7)),
        ],
        compiler_params=pltpu.CompilerParams(
            collective_id=0, has_side_effects=True, vmem_limit_bytes=60 * 2**20),
    )(cost, row_mass.reshape(1, ROWS), col_mass, slab)


def solution(mesh):
    return jax.shard_map(
        on_device,
        mesh=mesh,
        in_specs=(P("rows", "cols"), P("rows"), P("cols"), P("cols", None)),
        out_specs=P("rows", "cols"),
        check_vma=False,
    )
```

```python
import functools

import jax
import jax.numpy as jnp
from jax import lax
from jax.experimental import pallas as pl
from jax.experimental.pallas import tpu as pltpu
from jax.sharding import PartitionSpec as P

ITERS = 4
SHARPNESS = 80.0
MESH = pl.DeviceIdType.MESH
F32, BF16 = jnp.float32, jnp.bfloat16
NT = (((1,), (1,)), ((), ()))

ROWS, COLS, SLAB = 448, 3584, 512
NY = 8
OWN = SLAB // NY
CW = COLS // 2
TILES = CW // 128
TR = 16
LOADS = 7
LR = ROWS // LOADS
KC = 1792
PR = OWN // 4
BLOCKS = (4, 3, 5, 2, 6, 1, 7, 0)
ORDER = (4, 3, 5, 2, 6, 1, 7)
GROUP = tuple((other, dx, dz) for other in (0, 1) for dx, dz in
              ((2, 1), (2, 0), (1, 1), (3, 1), (1, 0), (3, 0), (0, 1), (0, 0)) if (other, dx, dz) != (0, 0, 0))


def parent(s):
    if abs(s) == 4:
        return s // 2
    return s + 1 if s < 0 else s - 1


def tree(p):
    left, right = (4, 3) if p % 2 == 0 else (3, 4)
    return [-s for s in range(left, 0, -1)] + list(range(right, 0, -1))


def split2(x):
    hi = x.astype(BF16).astype(F32)
    return hi, x - hi


def kernel(cost_ref, rm_hbm, cm_hbm, slab_ref, out_ref,
           k_ref, kt_ref, slab_v, slab_t, t_ref, rbuf, racc, over_ref, c2, left, rm_ref, cm_row, cm_ref,
           ysrc, ydst, xsrc, xdst, zsrc, zdst,
           cost_sem, slab_sem, mass_sem, ysend, yrecv, xsend, xrecv, zsend, zrecv, fsend, frecv):
    r = lax.axis_index("rows")
    y = lax.axis_index("cols")
    z = r // 8
    x = lax.rem(r, 8) // 2
    core = lax.rem(r, 2)
    odd = lax.rem(z, 2)
    sign = 2 * odd - 1

    def ypeer(d):
        return (r, lax.rem(y + d, 8))

    def place(to_z, to_x, to_core):
        return (to_z * 8 + to_x * 2 + to_core, y)

    def gpeer(other, dx, dz):
        to_core = core + other * (1 - 2 * core)
        return place(z - dz * sign, lax.rem(x + dx, 4), to_core)

    def zpeer(other, k):
        to_core = core + other * (1 - 2 * core)
        return place(lax.rem(z + k * sign + 8, 8), x, to_core)

    barrier = pltpu.get_barrier_semaphore()

    def greet(peer):
        pl.semaphore_signal(barrier, inc=1, device_id=peer, device_id_type=MESH)

    for d in ORDER:
        greet(ypeer(d))
    for other, dx, dz in GROUP:
        greet(gpeer(other, dx, dz))
    for k in (1, 2, 3, -2):
        for other in (0, 1):
            greet(zpeer(other, k))

    def load(i):
        s = pl.ds(i * LR, LR)
        return pltpu.make_async_copy(cost_ref.at[s], k_ref.at[s], cost_sem.at[i])

    for i in range(LOADS):
        load(i).start()
    rm_copy = pltpu.make_async_copy(rm_hbm, rm_ref, mass_sem.at[0])
    cm_copy = pltpu.make_async_copy(cm_hbm, cm_row, mass_sem.at[1])
    slab_copy = pltpu.make_async_copy(slab_ref, slab_v, slab_sem)
    rm_copy.start()
    cm_copy.start()
    slab_copy.start()

    left[...] = jnp.zeros_like(left)
    xsrc[...] = jnp.ones_like(xsrc)
    ysrc[...] = jnp.zeros_like(ysrc)
    cm_ref[...] = jnp.ones_like(cm_ref)

    for i in range(LOADS):
        load(i).wait()

        def exp_rows(j, carry, i=i):
            s = pl.ds(pl.multiple_of(i * LR + j * 32, 32), 32)
            k = jnp.exp(-SHARPNESS * k_ref[s, :].astype(F32)).astype(BF16)
            k_ref[s, :] = k
            k = k.astype(F32)
            total = k[:, 0:128]
            for q in range(1, COLS // 128):
                total = total + k[:, 128 * q:128 * (q + 1)]
            racc[s, :] = total
            return carry

        lax.fori_loop(0, LR // 32, exp_rows, 0)

    first = lax.dot_general(jnp.ones((8, 128), F32), racc[...], NT,
                            precision=lax.Precision.HIGHEST, preferred_element_type=F32)
    ysrc[0, :, 0:ROWS] = first[0:1]
    pl.semaphore_wait(barrier, 7 + len(GROUP) + 8)
    rm_copy.wait()
    cm_copy.wait()

    row8 = lax.broadcasted_iota(jnp.int32, (8, 1), 0)

    def two_rows(v):
        hi, rest = split2(v)
        return jnp.where(row8 == 0, hi, jnp.where(row8 == 1, rest, 0.0)).astype(BF16)

    def iteration(t, carry):
        for d in ORDER:
            pltpu.make_async_remote_copy(ysrc.at[t], ydst.at[t, d - 1], ysend.at[t], yrecv.at[t],
                                         device_id=ypeer(d), device_id_type=MESH).start()

        @pl.when(t == 0)
        def _():
            for h in range(2):
                for j in range(TILES):
                    cm_ref[h, j:j + 1, :] = cm_row[pl.ds(h * CW + 128 * j, 128)].reshape(1, 128)

            def turn(i, carry):
                s = pl.ds(pl.multiple_of(i * 512, 512), 512)
                kt_ref[s, :] = k_ref[:, s].T
                return carry

            lax.fori_loop(0, COLS // 512, turn, 0)

        pltpu.make_async_copy(ydst.at[t], ydst.at[t], yrecv.at[t]).wait()
        sums = ysrc[t, :, 0:ROWS]
        for d in range(7):
            sums = sums + ydst[t, d, :, 0:ROWS]
        r2 = two_rows(rm_ref[...] / sums)

        for other in (1, 0):
            h = core + other * (1 - 2 * core)
            part = jnp.dot(r2, k_ref[:, pl.ds(pl.multiple_of(h * CW, CW), CW)], preferred_element_type=F32)
            part = part[0:1] + part[1:2]
            for j in range(TILES):
                xsrc[t, other, j:j + 1, :] = part[:, 128 * j:128 * (j + 1)]
            for to, dx, dz in GROUP:
                if to == other:
                    pltpu.make_async_remote_copy(
                        xsrc.at[t, other], xdst.at[t, GROUP.index((to, dx, dz))], xsend.at[t], xrecv.at[t],
                        device_id=gpeer(to, dx, dz), device_id_type=MESH).start()

        @pl.when(t == ITERS - 1)
        def _():
            over_ref[...] = 1.0 / sums

        pltpu.make_async_copy(xdst.at[t], xdst.at[t], xrecv.at[t]).wait()
        total = xsrc[t, 0]
        for i in range(len(GROUP)):
            total = total + xdst[t, i]
        zsrc[t] = total
        for k, other in ((3, 1), (3, 0), (2, 1), (2, 0), (1, 1), (1, 0), (0, 1)):
            pltpu.make_async_remote_copy(zsrc.at[t], zdst.at[t, other, k], zsend.at[t], zrecv.at[t, other],
                                         device_id=zpeer(other, k), device_id_type=MESH).start()

        @pl.when(t == 0)
        def _():
            lane = lax.broadcasted_iota(jnp.int32, (SLAB, 1), 0)
            source = jnp.zeros((SLAB, 1), jnp.int32)
            for i, e in enumerate(BLOCKS):
                first_lane = lax.rem(y + e, 8) * OWN
                source = jnp.where(lane // OWN == i, first_lane + lane - i * OWN, source)
            moved = (lax.broadcasted_iota(jnp.int32, (SLAB, SLAB), 1) == source).astype(F32).astype(BF16)
            slab_copy.wait()

            def reorder(i, carry):
                s = pl.ds(pl.multiple_of(i * 512, 512), 512)
                slab_t[:, s] = lax.dot_general(moved, slab_v[s, :], NT, preferred_element_type=F32).astype(BF16)
                return carry

            lax.fori_loop(0, COLS // 512, reorder, 0)

        sums = jnp.zeros((8, ROWS), F32)
        for other in (0, 1):
            h = core + other * (1 - 2 * core)
            here = zdst.at[t, other, pl.ds(1 - other, 3 + other)]
            pltpu.make_async_copy(here, here, zrecv.at[t, other]).wait()
            total = zdst[t, other, 0] if other else zsrc[t]
            for k in (1, 2, 3):
                total = total + zdst[t, other, k]
            hi, rest = split2(cm_ref[h] / total)
            c2[0] = hi
            c2[1] = rest
            for j in range(TILES):
                lanes = pl.ds(pl.multiple_of(h * CW + 128 * j, 128), 128)
                left[0:1, lanes] = c2[0, j:j + 1, :]
                left[1:2, lanes] = c2[1, j:j + 1, :]
            lanes = pl.ds(pl.multiple_of(h * CW, CW), CW)
            part = jnp.dot(left[:, lanes].astype(BF16), kt_ref[lanes, :], preferred_element_type=F32)
            if other == 0:
                sums = part
            else:
                sums = sums + part

        @pl.when(t < ITERS - 1)
        def _():
            ysrc[t + 1, :, 0:ROWS] = sums[0:1] + sums[1:2]

        return carry

    lax.fori_loop(0, ITERS, iteration, 0)

    def piece(e, p):
        return pl.ds(BLOCKS.index(e % 8) * OWN + p * PR, PR)

    def hop(p, s):
        i = tree(p).index(s)
        return pltpu.make_async_remote_copy(
            t_ref.at[piece(-s, p)], rbuf.at[p, i], fsend.at[p, i], frecv.at[p, i],
            device_id=ypeer((parent(s) - s) % 8), device_id_type=MESH)

    def add_arrived(p, s, total):
        for child in tree(p):
            if parent(child) == s:
                i = tree(p).index(child)
                pltpu.make_async_copy(rbuf.at[p, i], rbuf.at[p, i], frecv.at[p, i]).wait()
                total = total + rbuf[p, i]
        return total

    for quarter in range(4):
        block_rows = slice(quarter * 128, quarter * 128 + 128)

        def product(i, carry, block_rows=block_rows):
            s = pl.ds(pl.multiple_of(i * KC, KC), KC)
            scale = left[0:1, s] + left[1:2, s]
            scaled = (slab_t[block_rows, s].astype(F32) * scale).astype(BF16)
            part = jnp.dot(scaled, kt_ref[s, :], preferred_element_type=F32)

            @pl.when(i == 0)
            def _():
                t_ref[block_rows, :] = part

            @pl.when(i > 0)
            def _():
                t_ref[block_rows, :] += part

            return carry

        lax.fori_loop(0, COLS // KC, product, 0)
        for m in ((4, -3), (3,), (), ())[quarter]:
            for p in range(4):
                for s in ((-4, 4) if m == 4 else (m,)):
                    if s in tree(p):
                        hop(p, s).start()

    for m in (2, 1):
        for p in range(4):
            for s in (-m, m):
                rows = piece(-s, p)
                t_ref[rows, :] = add_arrived(p, s, t_ref[rows, :])
                hop(p, s).start()
    for p in range(4):
        total = add_arrived(p, 0, t_ref[piece(0, p), :])
        out_ref[p * PR:(p + 1) * PR, :] = (total * over_ref[...]).astype(BF16)

    for t in range(ITERS):
        pltpu.make_async_copy(ydst.at[t], ydst.at[t], ysend.at[t]).wait()
        pltpu.make_async_copy(xdst.at[t], xdst.at[t], xsend.at[t]).wait()
        sent = zdst.at[t, 0, pl.ds(1, 3)]
        pltpu.make_async_copy(sent, sent, zsend.at[t]).wait()
        pltpu.make_async_copy(zdst.at[t, 1], zdst.at[t, 1], zsend.at[t]).wait()
    for p in range(4):
        for s in tree(p):
            hop(p, s).wait_send()


def on_device(cost, row_mass, col_mass, slab):
    hbm = pl.BlockSpec(memory_space=pltpu.HBM)
    dma = pltpu.SemaphoreType.DMA
    return pl.pallas_call(
        kernel,
        out_shape=jax.ShapeDtypeStruct((OWN, ROWS), BF16),
        in_specs=[hbm, hbm, hbm, hbm],
        out_specs=pl.BlockSpec(memory_space=pltpu.VMEM),
        scratch_shapes=[
            pltpu.VMEM((ROWS, COLS), BF16),
            pltpu.VMEM((COLS, ROWS), BF16),
            pltpu.VMEM((COLS, SLAB), BF16),
            pltpu.VMEM((SLAB, COLS), BF16),
            pltpu.VMEM((SLAB, ROWS), F32),
            pltpu.VMEM((4, 7, PR, ROWS), F32),
            pltpu.VMEM((ROWS, 128), F32),
            pltpu.VMEM((1, ROWS), F32),
            pltpu.VMEM((2, TR, 128), F32),
            pltpu.VMEM((8, COLS), F32),
            pltpu.VMEM((1, ROWS), F32),
            pltpu.VMEM((COLS,), F32),
            pltpu.VMEM((2, TR, 128), F32),
            pltpu.VMEM((ITERS, 1, 512), F32),
            pltpu.VMEM((ITERS, 7, 1, 512), F32),
            pltpu.VMEM((ITERS, 2, TR, 128), F32),
            pltpu.VMEM((ITERS, len(GROUP), TR, 128), F32),
            pltpu.VMEM((ITERS, TR, 128), F32),
            pltpu.VMEM((ITERS, 2, 4, TR, 128), F32),
            dma((LOADS,)), dma, dma((2,)),
            dma((ITERS,)), dma((ITERS,)),
            dma((ITERS,)), dma((ITERS,)),
            dma((ITERS,)), dma((ITERS, 2)),
            dma((4, 7)), dma((4, 7)),
        ],
        compiler_params=pltpu.CompilerParams(
            collective_id=0, has_side_effects=True, vmem_limit_bytes=60 * 2**20),
    )(cost, row_mass.reshape(1, ROWS), col_mass, slab).T


def solution(mesh):
    return jax.shard_map(
        on_device,
        mesh=mesh,
        in_specs=(P("rows", "cols"), P("rows"), P("cols"), P("cols", None)),
        out_specs=P("rows", "cols"),
        check_vma=False,
    )
```

```python
import functools

import jax
import jax.numpy as jnp
from jax import lax
from jax.experimental import pallas as pl
from jax.experimental.pallas import tpu as pltpu
from jax.sharding import PartitionSpec as P

ITERS = 4
SHARPNESS = 80.0
MESH = pl.DeviceIdType.MESH
F32, BF16 = jnp.float32, jnp.bfloat16
NT = (((1,), (1,)), ((), ()))

ROWS, COLS, SLAB = 448, 3584, 512
NY = 8
OWN = SLAB // NY
CW = COLS // 2
TILES = CW // 128
TR = 16
LOADS = 7
LR = ROWS // LOADS
KC = 1792
PR = OWN // 4
BLOCKS = (4, 3, 5, 2, 6, 1, 7, 0)
ORDER = (4, 3, 5, 2, 6, 1, 7)
GROUP = tuple((other, dx, dz) for other in (0, 1) for dx, dz in
              ((2, 1), (2, 0), (1, 1), (3, 1), (1, 0), (3, 0), (0, 1), (0, 0)) if (other, dx, dz) != (0, 0, 0))
FARTHEST = sorted(range(len(GROUP)), key=lambda i: -2 * (2 - abs(GROUP[i][1] - 2)) - GROUP[i][2])


def parent(s):
    if abs(s) == 4:
        return s // 2
    return s + 1 if s < 0 else s - 1


def tree(p):
    left, right = (4, 3) if p % 2 == 0 else (3, 4)
    return [-s for s in range(left, 0, -1)] + list(range(right, 0, -1))


def split2(x):
    hi = x.astype(BF16).astype(F32)
    return hi, x - hi


def kernel(cost_ref, rm_hbm, cm_hbm, slab_ref, out_ref,
           k_ref, kt_ref, slab_v, slab_t, t_ref, rbuf, racc, over_ref, c2, left, rm_ref, cm_row, cm_ref,
           ysrc, ydst, xsrc, xdst, zsrc, zdst,
           cost_sem, slab_sem, mass_sem, ysend, yrecv, xsend, xrecv, zsend, zrecv, fsend, frecv):
    r = lax.axis_index("rows")
    y = lax.axis_index("cols")
    z = r // 8
    x = lax.rem(r, 8) // 2
    core = lax.rem(r, 2)
    odd = lax.rem(z, 2)
    sign = 2 * odd - 1

    def ypeer(d):
        return (r, lax.rem(y + d, 8))

    def place(to_z, to_x, to_core):
        return (to_z * 8 + to_x * 2 + to_core, y)

    def gpeer(other, dx, dz):
        to_core = core + other * (1 - 2 * core)
        return place(z - dz * sign, lax.rem(x + dx, 4), to_core)

    def zpeer(other, k):
        to_core = core + other * (1 - 2 * core)
        return place(lax.rem(z + k * sign + 8, 8), x, to_core)

    barrier = pltpu.get_barrier_semaphore()

    def greet(peer):
        pl.semaphore_signal(barrier, inc=1, device_id=peer, device_id_type=MESH)

    for d in ORDER:
        greet(ypeer(d))
    for other, dx, dz in GROUP:
        greet(gpeer(other, dx, dz))
    for k in (1, 2, 3, -2):
        for other in (0, 1):
            greet(zpeer(other, k))

    def load(i):
        s = pl.ds(i * LR, LR)
        return pltpu.make_async_copy(cost_ref.at[s], k_ref.at[s], cost_sem.at[i])

    for i in range(LOADS):
        load(i).start()
    rm_copy = pltpu.make_async_copy(rm_hbm, rm_ref, mass_sem.at[0])
    cm_copy = pltpu.make_async_copy(cm_hbm, cm_row, mass_sem.at[1])
    slab_copy = pltpu.make_async_copy(slab_ref, slab_v, slab_sem)
    rm_copy.start()
    cm_copy.start()
    slab_copy.start()

    left[...] = jnp.zeros_like(left)
    xsrc[...] = jnp.ones_like(xsrc)
    ysrc[...] = jnp.zeros_like(ysrc)
    cm_ref[...] = jnp.ones_like(cm_ref)

    for i in range(LOADS):
        load(i).wait()

        def exp_rows(j, carry, i=i):
            s = pl.ds(pl.multiple_of(i * LR + j * 32, 32), 32)
            k = jnp.exp(-SHARPNESS * k_ref[s, :].astype(F32)).astype(BF16)
            k_ref[s, :] = k
            k = k.astype(F32)
            total = k[:, 0:128]
            for q in range(1, COLS // 128):
                total = total + k[:, 128 * q:128 * (q + 1)]
            racc[s, :] = total
            return carry

        lax.fori_loop(0, LR // 32, exp_rows, 0)

    first = lax.dot_general(jnp.ones((8, 128), F32), racc[...], NT,
                            precision=lax.Precision.HIGHEST, preferred_element_type=F32)
    ysrc[0, :, 0:ROWS] = first[0:1]
    pl.semaphore_wait(barrier, 7 + len(GROUP) + 8)
    rm_copy.wait()
    cm_copy.wait()

    row8 = lax.broadcasted_iota(jnp.int32, (8, 1), 0)

    def two_rows(v):
        hi, rest = split2(v)
        return jnp.where(row8 == 0, hi, jnp.where(row8 == 1, rest, 0.0)).astype(BF16)

    def iteration(t, carry):
        for d in ORDER:
            pltpu.make_async_remote_copy(ysrc.at[t], ydst.at[t, d - 1], ysend.at[t], yrecv.at[t],
                                         device_id=ypeer(d), device_id_type=MESH).start()

        @pl.when(t == 0)
        def _():
            for h in range(2):
                for j in range(TILES):
                    cm_ref[h, j:j + 1, :] = cm_row[pl.ds(h * CW + 128 * j, 128)].reshape(1, 128)

            def turn(i, carry):
                s = pl.ds(pl.multiple_of(i * 512, 512), 512)
                kt_ref[s, :] = k_ref[:, s].T
                return carry

            lax.fori_loop(0, COLS // 512, turn, 0)

        pltpu.make_async_copy(ydst.at[t], ydst.at[t], yrecv.at[t]).wait()
        sums = ysrc[t, :, 0:ROWS]
        for d in range(7):
            sums = sums + ydst[t, d, :, 0:ROWS]
        r2 = two_rows(rm_ref[...] / sums)

        part = jnp.dot(r2, k_ref[...], preferred_element_type=F32)
        part = part[0:1] + part[1:2]
        for h in (0, 1):
            for j in range(TILES):
                xsrc[t, h, j:j + 1, :] = part[:, h * CW + 128 * j:h * CW + 128 * (j + 1)]
        for i in FARTHEST:
            other, dx, dz = GROUP[i]
            h = core + other * (1 - 2 * core)
            pltpu.make_async_remote_copy(xsrc.at[t, h], xdst.at[t, i], xsend.at[t], xrecv.at[t],
                                         device_id=gpeer(other, dx, dz), device_id_type=MESH).start()

        @pl.when(t == ITERS - 1)
        def _():
            over_ref[...] = 1.0 / sums

        pltpu.make_async_copy(xdst.at[t], xdst.at[t], xrecv.at[t]).wait()
        total = xsrc[t, core]
        for i in range(len(GROUP)):
            total = total + xdst[t, i]
        zsrc[t] = total
        for k, other in ((3, 1), (3, 0), (2, 1), (2, 0), (1, 1), (1, 0), (0, 1)):
            pltpu.make_async_remote_copy(zsrc.at[t], zdst.at[t, other, k], zsend.at[t], zrecv.at[t, other],
                                         device_id=zpeer(other, k), device_id_type=MESH).start()

        @pl.when(t == 0)
        def _():
            lane = lax.broadcasted_iota(jnp.int32, (SLAB, 1), 0)
            source = jnp.zeros((SLAB, 1), jnp.int32)
            for i, e in enumerate(BLOCKS):
                first_lane = lax.rem(y + e, 8) * OWN
                source = jnp.where(lane // OWN == i, first_lane + lane - i * OWN, source)
            moved = (lax.broadcasted_iota(jnp.int32, (SLAB, SLAB), 1) == source).astype(F32).astype(BF16)
            slab_copy.wait()

            def reorder(i, carry):
                s = pl.ds(pl.multiple_of(i * 512, 512), 512)
                slab_t[:, s] = lax.dot_general(moved, slab_v[s, :], NT, preferred_element_type=F32).astype(BF16)
                return carry

            lax.fori_loop(0, COLS // 512, reorder, 0)

        sums = jnp.zeros((8, ROWS), F32)
        for other in (0, 1):
            h = core + other * (1 - 2 * core)
            here = zdst.at[t, other, pl.ds(1 - other, 3 + other)]
            pltpu.make_async_copy(here, here, zrecv.at[t, other]).wait()
            total = zdst[t, other, 0] if other else zsrc[t]
            for k in (1, 2, 3):
                total = total + zdst[t, other, k]
            hi, rest = split2(cm_ref[h] / total)
            c2[0] = hi
            c2[1] = rest
            for j in range(TILES):
                lanes = pl.ds(pl.multiple_of(h * CW + 128 * j, 128), 128)
                left[0:1, lanes] = c2[0, j:j + 1, :]
                left[1:2, lanes] = c2[1, j:j + 1, :]
            lanes = pl.ds(pl.multiple_of(h * CW, CW), CW)
            part = jnp.dot(left[:, lanes].astype(BF16), kt_ref[lanes, :], preferred_element_type=F32)
            if other == 0:
                sums = part
            else:
                sums = sums + part

        @pl.when(t < ITERS - 1)
        def _():
            ysrc[t + 1, :, 0:ROWS] = sums[0:1] + sums[1:2]

        return carry

    lax.fori_loop(0, ITERS, iteration, 0)

    def piece(e, p):
        return pl.ds(BLOCKS.index(e % 8) * OWN + p * PR, PR)

    def hop(p, s):
        i = tree(p).index(s)
        return pltpu.make_async_remote_copy(
            t_ref.at[piece(-s, p)], rbuf.at[p, i], fsend.at[p, i], frecv.at[p, i],
            device_id=ypeer((parent(s) - s) % 8), device_id_type=MESH)

    def add_arrived(p, s, total):
        for child in tree(p):
            if parent(child) == s:
                i = tree(p).index(child)
                pltpu.make_async_copy(rbuf.at[p, i], rbuf.at[p, i], frecv.at[p, i]).wait()
                total = total + rbuf[p, i]
        return total

    for quarter in range(4):
        block_rows = slice(quarter * 128, quarter * 128 + 128)

        def product(i, carry, block_rows=block_rows):
            s = pl.ds(pl.multiple_of(i * KC, KC), KC)
            scale = left[0:1, s] + left[1:2, s]
            scaled = (slab_t[block_rows, s].astype(F32) * scale).astype(BF16)
            part = jnp.dot(scaled, kt_ref[s, :], preferred_element_type=F32)

            @pl.when(i == 0)
            def _():
                t_ref[block_rows, :] = part

            @pl.when(i > 0)
            def _():
                t_ref[block_rows, :] += part

            return carry

        lax.fori_loop(0, COLS // KC, product, 0)
        for m in ((4, -3), (3,), (), ())[quarter]:
            for p in range(4):
                for s in ((-4, 4) if m == 4 else (m,)):
                    if s in tree(p):
                        hop(p, s).start()

    for m in (2, 1):
        for p in range(4):
            for s in (-m, m):
                rows = piece(-s, p)
                t_ref[rows, :] = add_arrived(p, s, t_ref[rows, :])
                hop(p, s).start()
    for p in range(4):
        total = add_arrived(p, 0, t_ref[piece(0, p), :])
        out_ref[p * PR:(p + 1) * PR, :] = (total * over_ref[...]).astype(BF16)

    for t in range(ITERS):
        pltpu.make_async_copy(ydst.at[t], ydst.at[t], ysend.at[t]).wait()
        pltpu.make_async_copy(xdst.at[t], xdst.at[t], xsend.at[t]).wait()
        sent = zdst.at[t, 0, pl.ds(1, 3)]
        pltpu.make_async_copy(sent, sent, zsend.at[t]).wait()
        pltpu.make_async_copy(zdst.at[t, 1], zdst.at[t, 1], zsend.at[t]).wait()
    for p in range(4):
        for s in tree(p):
            hop(p, s).wait_send()


def on_device(cost, row_mass, col_mass, slab):
    hbm = pl.BlockSpec(memory_space=pltpu.HBM)
    dma = pltpu.SemaphoreType.DMA
    return pl.pallas_call(
        kernel,
        out_shape=pltpu.VMEM((OWN, ROWS), BF16),
        in_specs=[hbm, hbm, hbm, hbm],
        out_specs=pl.BlockSpec(memory_space=pltpu.VMEM),
        scratch_shapes=[
            pltpu.VMEM((ROWS, COLS), BF16),
            pltpu.VMEM((COLS, ROWS), BF16),
            pltpu.VMEM((COLS, SLAB), BF16),
            pltpu.VMEM((SLAB, COLS), BF16),
            pltpu.VMEM((SLAB, ROWS), F32),
            pltpu.VMEM((4, 7, PR, ROWS), F32),
            pltpu.VMEM((ROWS, 128), F32),
            pltpu.VMEM((1, ROWS), F32),
            pltpu.VMEM((2, TR, 128), F32),
            pltpu.VMEM((8, COLS), F32),
            pltpu.VMEM((1, ROWS), F32),
            pltpu.VMEM((COLS,), F32),
            pltpu.VMEM((2, TR, 128), F32),
            pltpu.VMEM((ITERS, 1, 512), F32),
            pltpu.VMEM((ITERS, 7, 1, 512), F32),
            pltpu.VMEM((ITERS, 2, TR, 128), F32),
            pltpu.VMEM((ITERS, len(GROUP), TR, 128), F32),
            pltpu.VMEM((ITERS, TR, 128), F32),
            pltpu.VMEM((ITERS, 2, 4, TR, 128), F32),
            dma((LOADS,)), dma, dma((2,)),
            dma((ITERS,)), dma((ITERS,)),
            dma((ITERS,)), dma((ITERS,)),
            dma((ITERS,)), dma((ITERS, 2)),
            dma((4, 7)), dma((4, 7)),
        ],
        compiler_params=pltpu.CompilerParams(
            collective_id=0, has_side_effects=True, vmem_limit_bytes=60 * 2**20),
    )(cost, row_mass.reshape(1, ROWS), col_mass, slab).T


def solution(mesh):
    return jax.shard_map(
        on_device,
        mesh=mesh,
        in_specs=(P("rows", "cols"), P("rows"), P("cols"), P("cols", None)),
        out_specs=P("rows", "cols"),
        check_vma=False,
    )
```

```python
import functools

import jax
import jax.numpy as jnp
from jax import lax
from jax.experimental import pallas as pl
from jax.experimental.pallas import tpu as pltpu
from jax.sharding import PartitionSpec as P

ITERS = 4
SHARPNESS = 80.0
MESH = pl.DeviceIdType.MESH
F32, BF16 = jnp.float32, jnp.bfloat16
NT = (((1,), (1,)), ((), ()))

ROWS, COLS, SLAB = 448, 3584, 512
NY = 8
OWN = SLAB // NY
CW = COLS // 2
TILES = CW // 128
TR = 16
LOADS = 7
LR = ROWS // LOADS
KC = 1792
PR = OWN // 4
BLOCKS = (4, 3, 5, 2, 6, 1, 7, 0)
ORDER = (4, 3, 5, 2, 6, 1, 7)
GROUP = tuple((other, dx, dz) for other in (0, 1) for dx, dz in
              ((2, 1), (2, 0), (1, 1), (3, 1), (1, 0), (3, 0), (0, 1), (0, 0)) if (other, dx, dz) != (0, 0, 0))
FARTHEST = sorted(range(len(GROUP)), key=lambda i: -2 * (2 - abs(GROUP[i][1] - 2)) - GROUP[i][2])


def parent(s):
    if abs(s) == 4:
        return s // 2
    return s + 1 if s < 0 else s - 1


def tree(p):
    left, right = (4, 3) if p % 2 == 0 else (3, 4)
    return [-s for s in range(left, 0, -1)] + list(range(right, 0, -1))


def split2(x):
    hi = x.astype(BF16).astype(F32)
    return hi, x - hi


def kernel(cost_ref, rm_hbm, cm_hbm, slab_ref, out_ref,
           k_ref, kt_ref, slab_v, slab_t, t_ref, rbuf, racc, over_ref, c2, left, rm_ref, cm_row, cm_ref,
           ysrc, ydst, xsrc, xdst, zsrc, zdst,
           cost_sem, slab_sem, mass_sem, ysend, yrecv, xsend, xrecv, zsend, zrecv, fsend, frecv):
    r = lax.axis_index("rows")
    y = lax.axis_index("cols")
    z = r // 8
    x = lax.rem(r, 8) // 2
    core = lax.rem(r, 2)
    odd = lax.rem(z, 2)
    sign = 2 * odd - 1

    def ypeer(d):
        return (r, lax.rem(y + d, 8))

    def place(to_z, to_x, to_core):
        return (to_z * 8 + to_x * 2 + to_core, y)

    def gpeer(other, dx, dz):
        to_core = core + other * (1 - 2 * core)
        return place(z - dz * sign, lax.rem(x + dx, 4), to_core)

    def zpeer(other, k):
        to_core = core + other * (1 - 2 * core)
        return place(lax.rem(z + k * sign + 8, 8), x, to_core)

    barrier = pltpu.get_barrier_semaphore()

    def greet(peer):
        pl.semaphore_signal(barrier, inc=1, device_id=peer, device_id_type=MESH)

    for d in ORDER:
        greet(ypeer(d))
    for other, dx, dz in GROUP:
        greet(gpeer(other, dx, dz))
    for k in (1, 2, 3, -2):
        for other in (0, 1):
            greet(zpeer(other, k))

    def load(i):
        s = pl.ds(i * LR, LR)
        return pltpu.make_async_copy(cost_ref.at[s], k_ref.at[s], cost_sem.at[i])

    for i in range(LOADS):
        load(i).start()
    rm_copy = pltpu.make_async_copy(rm_hbm, rm_ref, mass_sem.at[0])
    cm_copy = pltpu.make_async_copy(cm_hbm, cm_row, mass_sem.at[1])
    slab_copy = pltpu.make_async_copy(slab_ref, slab_v, slab_sem)
    rm_copy.start()
    cm_copy.start()
    slab_copy.start()

    left[...] = jnp.zeros_like(left)
    xsrc[...] = jnp.ones_like(xsrc)
    ysrc[...] = jnp.zeros_like(ysrc)
    cm_ref[...] = jnp.ones_like(cm_ref)

    for i in range(LOADS):
        load(i).wait()

        def exp_rows(j, carry, i=i):
            s = pl.ds(pl.multiple_of(i * LR + j * 32, 32), 32)
            k = jnp.exp(-SHARPNESS * k_ref[s, :].astype(F32)).astype(BF16)
            k_ref[s, :] = k
            k = k.astype(F32)
            total = k[:, 0:128]
            for q in range(1, COLS // 128):
                total = total + k[:, 128 * q:128 * (q + 1)]
            racc[s, :] = total
            return carry

        lax.fori_loop(0, LR // 32, exp_rows, 0)

    first = lax.dot_general(jnp.ones((8, 128), F32), racc[...], NT,
                            precision=lax.Precision.HIGHEST, preferred_element_type=F32)
    ysrc[0, :, 0:ROWS] = first[0:1]
    pl.semaphore_wait(barrier, 7 + len(GROUP) + 8)
    rm_copy.wait()
    cm_copy.wait()

    row8 = lax.broadcasted_iota(jnp.int32, (8, 1), 0)

    def two_rows(v):
        hi, rest = split2(v)
        return jnp.where(row8 == 0, hi, jnp.where(row8 == 1, rest, 0.0)).astype(BF16)

    def iteration(t, carry):
        for d in ORDER:
            pltpu.make_async_remote_copy(ysrc.at[t], ydst.at[t, d - 1], ysend.at[t], yrecv.at[t],
                                         device_id=ypeer(d), device_id_type=MESH).start()

        @pl.when(t == 0)
        def _():
            for h in range(2):
                for j in range(TILES):
                    cm_ref[h, j:j + 1, :] = cm_row[pl.ds(h * CW + 128 * j, 128)].reshape(1, 128)

            def turn(i, carry):
                s = pl.ds(pl.multiple_of(i * 512, 512), 512)
                kt_ref[s, :] = k_ref[:, s].T
                return carry

            lax.fori_loop(0, COLS // 512, turn, 0)

        pltpu.make_async_copy(ydst.at[t], ydst.at[t], yrecv.at[t]).wait()
        sums = ysrc[t, :, 0:ROWS]
        for d in range(7):
            sums = sums + ydst[t, d, :, 0:ROWS]
        r2 = two_rows(rm_ref[...] / sums)

        part = jnp.dot(r2, k_ref[...], preferred_element_type=F32)
        part = part[0:1] + part[1:2]
        for h in (0, 1):
            for j in range(TILES):
                xsrc[t, h, j:j + 1, :] = part[:, h * CW + 128 * j:h * CW + 128 * (j + 1)]
        for i in FARTHEST:
            other, dx, dz = GROUP[i]
            h = core + other * (1 - 2 * core)
            pltpu.make_async_remote_copy(xsrc.at[t, h], xdst.at[t, i], xsend.at[t], xrecv.at[t],
                                         device_id=gpeer(other, dx, dz), device_id_type=MESH).start()

        @pl.when(t == ITERS - 1)
        def _():
            over_ref[...] = 1.0 / sums

        pltpu.make_async_copy(xdst.at[t], xdst.at[t], xrecv.at[t]).wait()
        total = xsrc[t, core]
        for i in range(len(GROUP)):
            total = total + xdst[t, i]
        zsrc[t] = total
        for k, other in ((3, 1), (3, 0), (2, 1), (2, 0), (1, 1), (1, 0), (0, 1)):
            pltpu.make_async_remote_copy(zsrc.at[t], zdst.at[t, other, k], zsend.at[t], zrecv.at[t, other],
                                         device_id=zpeer(other, k), device_id_type=MESH).start()

        @pl.when(t == 0)
        def _():
            lane = lax.broadcasted_iota(jnp.int32, (SLAB, 1), 0)
            source = jnp.zeros((SLAB, 1), jnp.int32)
            for i, e in enumerate(BLOCKS):
                first_lane = lax.rem(y + e, 8) * OWN
                source = jnp.where(lane // OWN == i, first_lane + lane - i * OWN, source)
            moved = (lax.broadcasted_iota(jnp.int32, (SLAB, SLAB), 1) == source).astype(F32).astype(BF16)
            slab_copy.wait()

            def reorder(i, carry):
                s = pl.ds(pl.multiple_of(i * 512, 512), 512)
                slab_t[:, s] = lax.dot_general(moved, slab_v[s, :], NT, preferred_element_type=F32).astype(BF16)
                return carry

            lax.fori_loop(0, COLS // 512, reorder, 0)

        for other in (0, 1):
            h = core + other * (1 - 2 * core)
            here = zdst.at[t, other, pl.ds(1 - other, 3 + other)]
            pltpu.make_async_copy(here, here, zrecv.at[t, other]).wait()
            total = zdst[t, other, 0] if other else zsrc[t]
            for k in (1, 2, 3):
                total = total + zdst[t, other, k]
            hi, rest = split2(cm_ref[h] / total)
            c2[0] = hi
            c2[1] = rest
            for j in range(TILES):
                lanes = pl.ds(pl.multiple_of(h * CW + 128 * j, 128), 128)
                left[0:1, lanes] = c2[0, j:j + 1, :]
                left[1:2, lanes] = c2[1, j:j + 1, :]

        @pl.when(t < ITERS - 1)
        def _():
            sums = jnp.dot(left[...].astype(BF16), kt_ref[...], preferred_element_type=F32)
            ysrc[t + 1, :, 0:ROWS] = sums[0:1] + sums[1:2]

        return carry

    lax.fori_loop(0, ITERS, iteration, 0)

    def piece(e, p):
        return pl.ds(BLOCKS.index(e % 8) * OWN + p * PR, PR)

    def hop(p, s):
        i = tree(p).index(s)
        return pltpu.make_async_remote_copy(
            t_ref.at[piece(-s, p)], rbuf.at[p, i], fsend.at[p, i], frecv.at[p, i],
            device_id=ypeer((parent(s) - s) % 8), device_id_type=MESH)

    def add_arrived(p, s, total):
        for child in tree(p):
            if parent(child) == s:
                i = tree(p).index(child)
                pltpu.make_async_copy(rbuf.at[p, i], rbuf.at[p, i], frecv.at[p, i]).wait()
                total = total + rbuf[p, i]
        return total

    for quarter in range(4):
        block_rows = slice(quarter * 128, quarter * 128 + 128)

        def product(i, carry, block_rows=block_rows):
            s = pl.ds(pl.multiple_of(i * KC, KC), KC)
            scale = left[0:1, s] + left[1:2, s]
            scaled = (slab_t[block_rows, s].astype(F32) * scale).astype(BF16)
            part = jnp.dot(scaled, kt_ref[s, :], preferred_element_type=F32)

            @pl.when(i == 0)
            def _():
                t_ref[block_rows, :] = part

            @pl.when(i > 0)
            def _():
                t_ref[block_rows, :] += part

            return carry

        lax.fori_loop(0, COLS // KC, product, 0)
        for m in ((4, -3), (3,), (), ())[quarter]:
            for p in range(4):
                for s in ((-4, 4) if m == 4 else (m,)):
                    if s in tree(p):
                        hop(p, s).start()

    for m in (2, 1):
        for p in range(4):
            for s in (-m, m):
                rows = piece(-s, p)
                t_ref[rows, :] = add_arrived(p, s, t_ref[rows, :])
                hop(p, s).start()
    for p in range(4):
        total = add_arrived(p, 0, t_ref[piece(0, p), :])
        out_ref[p * PR:(p + 1) * PR, :] = (total * over_ref[...]).astype(BF16)

    for t in range(ITERS):
        pltpu.make_async_copy(ydst.at[t], ydst.at[t], ysend.at[t]).wait()
        pltpu.make_async_copy(xdst.at[t], xdst.at[t], xsend.at[t]).wait()
        sent = zdst.at[t, 0, pl.ds(1, 3)]
        pltpu.make_async_copy(sent, sent, zsend.at[t]).wait()
        pltpu.make_async_copy(zdst.at[t, 1], zdst.at[t, 1], zsend.at[t]).wait()
    for p in range(4):
        for s in tree(p):
            hop(p, s).wait_send()


def on_device(cost, row_mass, col_mass, slab):
    hbm = pl.BlockSpec(memory_space=pltpu.HBM)
    dma = pltpu.SemaphoreType.DMA
    return pl.pallas_call(
        kernel,
        out_shape=pltpu.VMEM((OWN, ROWS), BF16),
        in_specs=[hbm, hbm, hbm, hbm],
        out_specs=pl.BlockSpec(memory_space=pltpu.VMEM),
        scratch_shapes=[
            pltpu.VMEM((ROWS, COLS), BF16),
            pltpu.VMEM((COLS, ROWS), BF16),
            pltpu.VMEM((COLS, SLAB), BF16),
            pltpu.VMEM((SLAB, COLS), BF16),
            pltpu.VMEM((SLAB, ROWS), F32),
            pltpu.VMEM((4, 7, PR, ROWS), F32),
            pltpu.VMEM((ROWS, 128), F32),
            pltpu.VMEM((1, ROWS), F32),
            pltpu.VMEM((2, TR, 128), F32),
            pltpu.VMEM((8, COLS), F32),
            pltpu.VMEM((1, ROWS), F32),
            pltpu.VMEM((COLS,), F32),
            pltpu.VMEM((2, TR, 128), F32),
            pltpu.VMEM((ITERS, 1, 512), F32),
            pltpu.VMEM((ITERS, 7, 1, 512), F32),
            pltpu.VMEM((ITERS, 2, TR, 128), F32),
            pltpu.VMEM((ITERS, len(GROUP), TR, 128), F32),
            pltpu.VMEM((ITERS, TR, 128), F32),
            pltpu.VMEM((ITERS, 2, 4, TR, 128), F32),
            dma((LOADS,)), dma, dma((2,)),
            dma((ITERS,)), dma((ITERS,)),
            dma((ITERS,)), dma((ITERS,)),
            dma((ITERS,)), dma((ITERS, 2)),
            dma((4, 7)), dma((4, 7)),
        ],
        compiler_params=pltpu.CompilerParams(
            collective_id=0, has_side_effects=True, vmem_limit_bytes=60 * 2**20),
    )(cost, row_mass.reshape(1, ROWS), col_mass, slab).T


def solution(mesh):
    return jax.shard_map(
        on_device,
        mesh=mesh,
        in_specs=(P("rows", "cols"), P("rows"), P("cols"), P("cols", None)),
        out_specs=P("rows", "cols"),
        check_vma=False,
    )
```
